32 devices in a mesh: prompt: 2 (over x), feat: 16 (over z, y, core).
Axes of the slice: x: 2, y: 2, z: 4, core: 2. Of those that a mesh axis runs over, the one named last changes fastest.
Arguments:
- decoder: bfloat16 [4096, 5376], P('feat'), may hold values from -0.078125 to 0.078125
- encoder: bfloat16 [12288, 5376], P(('feat', 'prompt')), may hold values from -6 to 6
- row_ids: int32 [2, 256], P('prompt', 'feat'), may hold values from 0 to 255
- counts: int32 [2, 16], P('prompt'), may hold values from 1 to 16, 153 in all within a row
- activity: float32 [2, 256], P('prompt'), may hold values from 0.25 to 4
Outputs:
- edges: bfloat16 [2, 256, 12288], P('prompt', None, 'feat')
The draws below stay inside these ranges and needn't reach their ends.
Inputs may be any that keep to these rules, and one draw needn't show every extreme that they name: counts of one prompt sum to 153; some owner of each prompt holds exactly 16.
All inputs are finite; a program needn't handle non-finite values.
Results may differ from the reference program's by a relative error of at most 0.001.
Values may be sent and summed in bfloat16 or wider, within the bound.
A program may use at most 64 MiB of HBM per device.

```python
import math
import jax
import jax.numpy as jnp
import numpy as np
from jax import lax

D = 5376
OWN_CAP = 16
SRC_DEV = 256
PROMPTS = 2
SLOTS = 256
FILLED = 153
FT = 12288
NSRC = 4096
N_FEAT = 16


def plant(values, key, least, top_value):
    longest = values.shape.index(max(values.shape))
    spots = []
    for shift in (0, 1):
        where = [jax.random.randint(jax.random.fold_in(key, axis), (), 0, length) for axis, length in enumerate(values.shape)]
        where[longest] = (where[longest] + shift) % values.shape[longest]
        spots.append(tuple(where))
    return values.at[spots[0]].set(least).at[spots[1]].set(top_value)


def block_scale(key, extent, split, smallest, top_value):
    level = 1.0
    for axis_at, shards_of in split:
        heights = jax.random.uniform(jax.random.fold_in(jax.random.fold_in(key, 6), axis_at), (shards_of,), jnp.float32, smallest / len(split), top_value / len(split))
        level = level * jnp.repeat(jnp.exp(heights), extent[axis_at] // shards_of).reshape((-1,) + (1,) * (len(extent) - 1 - axis_at))
    return level


def length_profile(count, total, bound, slope):
    loads = [(1 << 20) // math.isqrt(grade ** slope) + 1 for grade in range(2, count + 1)]
    spare, given = total - bound - (count - 1), [1] * (count - 1)
    while spare > 0:
        movable = [i for i in range(count - 1) if given[i] < bound]
        pool, remaining = sum([loads[i] for i in movable]), spare
        for i in movable:
            more = min(bound - given[i], max(1, remaining * loads[i] // pool), spare)
            given[i] = given[i] + more
            spare = spare - more
    return np.array([bound] + given)


def ragged(stream_key, count, total, bound, slope):
    if count == 2:
        one = jax.random.randint(stream_key, (), max(1, total - bound), min(bound, total - 1) + 1)
        return jnp.stack([one, total - one])
    tallies = jnp.asarray(length_profile(count, total, bound, slope), jnp.int32)
    twos = (count - 1) // 2
    donor, receiver = tallies[1:1 + 2 * twos:2], tallies[2:2 + 2 * twos:2]
    room = jnp.minimum(donor - 1, bound - receiver)
    moved = jax.random.randint(jax.random.fold_in(stream_key, 1), (twos,), 0, 1 << 20) % (room + 1)
    tallies = tallies.at[1:1 + 2 * twos:2].set(donor - moved).at[2:2 + 2 * twos:2].set(receiver + moved)
    return tallies[jax.random.permutation(jax.random.fold_in(stream_key, 2), count)]


def bell_draw(own_key, dims, spread, bound, cuts=(), held_as=jnp.bfloat16):
    values = jax.random.normal(own_key, dims, jnp.float32) * spread
    if len(cuts) > 0:
        values = block_scale(own_key, dims, cuts, -0.22, 0.18) * values
    return jnp.clip(values, min=-bound, max=bound).astype(held_as)


def setup_inputs(seed: int = 0) -> dict:
    key_of = jax.random.split(jax.random.key(seed), 6)
    decoder = bell_draw(key_of[0], (NSRC, D), D ** -0.5, 0.078125, ((0, 16),))
    encoder = bell_draw(key_of[1], (FT, D), 1.0, 6.0, ((0, 32),))
    row_ids = plant(jax.random.randint(key_of[2], (PROMPTS, SLOTS), 0, SRC_DEV), jax.random.fold_in(key_of[2], 1), 0, SRC_DEV - 1).astype(jnp.int32)
    counts = jax.vmap(lambda own: ragged(own, N_FEAT, FILLED, OWN_CAP, 2))(jax.random.split(key_of[3], PROMPTS)).reshape((PROMPTS, N_FEAT)).astype(jnp.int32)
    activity = jnp.clip(jnp.exp(math.log(4.0) - 2.7725887 * jax.random.uniform(key_of[4], (PROMPTS, SLOTS), jnp.float32) ** block_scale(key_of[4], (PROMPTS, SLOTS), ((0, 2),), -0.2, 0.2)), 0.25, 4.0)
    return {"decoder": decoder, "encoder": encoder, "row_ids": row_ids, "counts": counts, "activity": activity}


def reference(decoder, encoder, row_ids, counts, activity):
    owner_index = jnp.repeat(jnp.arange(N_FEAT, dtype=jnp.int32), OWN_CAP)
    slot_index = jnp.tile(jnp.arange(OWN_CAP, dtype=jnp.int32), N_FEAT)

    def per_prompt(inputs):
        local_ids, owner_counts, weights = inputs
        global_ids = (owner_index * SRC_DEV + local_ids).astype(jnp.int32)
        live_slots = slot_index < jnp.repeat(owner_counts, OWN_CAP)
        source_rows = jnp.where(live_slots[:, None], decoder[global_ids], jnp.zeros((), decoder.dtype))
        products = jnp.dot(source_rows, encoder.T, preferred_element_type=jnp.float32)
        return (weights[:, None] * products).astype(jnp.bfloat16)

    return lax.map(per_prompt, (row_ids, counts, activity))
```

```python
import functools

import jax
import jax.numpy as jnp
from jax import lax
from jax.experimental import pallas as pl
from jax.experimental.pallas import tpu as pltpu
from jax.sharding import PartitionSpec as P

MESH = pl.DeviceIdType.MESH
LANES = 128
COLUMNS = 2
CORES = 2


def gathered_encoder(decoder, encoder, row_ids, counts, activity):
    slot_count = row_ids.shape[1]
    owner_index = lax.axis_index("feat")
    picked_rows = jnp.take(decoder, row_ids[0], axis=0)
    live_count = lax.dynamic_index_in_dim(counts[0], owner_index, 0, keepdims=False)
    live_slots = jnp.arange(slot_count, dtype=jnp.int32) < live_count
    source_rows = jnp.where(live_slots[:, None], picked_rows, jnp.zeros((), picked_rows.dtype))
    weights = activity[0]
    whole_rows = lax.all_gather(source_rows, "feat", axis=0, tiled=True)
    products = lax.dot_general(
        whole_rows,
        lax.all_gather(encoder, "prompt", axis=0, tiled=True),
        (((1,), (1,)), ((), ())),
        preferred_element_type=jnp.float32,
    )
    edges = (weights[:, None] * products).astype(jnp.bfloat16)
    return edges[None]


X, Y, UP, DOWN, SIB = range(5)


def kernel(
    layers, ids_ref, counts_ref, act_ref, dec_hbm, enc_hbm, out_ref,
    buf, dec, enc, act_other, part, local_sem, pair_send, pair_recv, send_sem, recv_sem,
):
    own, width = buf.shape[2], buf.shape[3]
    targets = enc.shape[0]
    slots = buf.shape[1] * own
    half_width = width // LANES // 2 * LANES
    spans = (pl.ds(0, half_width), pl.ds(half_width, width - half_width))

    p = lax.axis_index("prompt")
    f = lax.axis_index("feat")
    core = f % CORES
    y = (f // CORES) % COLUMNS
    z = f // (CORES * COLUMNS)
    q, yo = 1 - p, 1 - y

    def owner(layer, column, which=None):
        return (layer * COLUMNS + column) * CORES + (core if which is None else which)

    places = {
        X: (q, f),
        Y: (p, owner(z, yo)),
        UP: (p, owner(z + 1, y)),
        DOWN: (p, owner(z - 1, y)),
        SIB: (p, owner(z, y, 1 - core)),
    }
    inside = {UP: z < layers - 1, DOWN: z > 0}

    load_dec = pltpu.make_async_copy(dec_hbm, dec, local_sem.at[0])
    load_enc = pltpu.make_async_copy(enc_hbm, enc, local_sem.at[1])
    load_dec.start()

    barrier = pltpu.get_barrier_semaphore()
    for way in (X, Y, SIB):
        pl.semaphore_signal(barrier, inc=1, device_id=places[way], device_id_type=MESH)
    for way in (UP, DOWN):
        @pl.when(inside[way])
        def _():
            pl.semaphore_signal(barrier, inc=1, device_id=places[way], device_id_type=MESH)

    row_count = dec.shape[0]
    lane = lax.broadcasted_iota(jnp.int32, (own, row_count), 1)
    slot = lax.broadcasted_iota(jnp.int32, (own, row_count), 0)
    live = counts_ref[0, f]
    wanted = jnp.full((own, row_count), -1, jnp.int32)
    for k in range(own):
        wanted = jnp.where(slot == k, jnp.where(k < live, ids_ref[0, k], -1), wanted)
    one_hot = jnp.where(lane == wanted, 1.0, 0.0).astype(jnp.bfloat16)
    load_dec.wait()
    load_enc.start()
    for span in spans:
        picked = jnp.dot(one_hot, dec[:, span], preferred_element_type=jnp.float32)
        buf[p, f, :, span] = picked.astype(buf.dtype)

    peers = 3 + (z + layers - 1) // layers + (layers - 1 - z + layers - 1) // layers
    pl.semaphore_wait(barrier, peers)

    started = []

    def piece(half, prompt, unit, way):
        ref = buf.at[prompt, unit, :, spans[half]]
        return pltpu.make_async_remote_copy(
            src_ref=ref, dst_ref=ref,
            send_sem=send_sem.at[way, half, prompt, unit],
            recv_sem=recv_sem.at[half, prompt, unit],
            device_id=places[way], device_id_type=MESH,
        )

    def send(half, prompt, unit, way, guard=None):
        copy = piece(half, prompt, unit, way)
        started.append((guard, copy))
        if guard is None:
            copy.start()
        else:
            pl.when(guard)(copy.start)

    def arrived(half, prompt, unit):
        piece(half, prompt, unit, SIB).wait_recv()

    def both(a, b):
        return jnp.logical_and(a, b)

    act_copy = pltpu.make_async_remote_copy(
        src_ref=act_ref, dst_ref=act_other, send_sem=pair_send.at[0], recv_sem=pair_recv.at[0],
        device_id=places[X], device_id_type=MESH,
    )
    act_copy.start()

    last = (X, Y)
    send(0, p, f, Y)
    send(1, p, f, X)
    for way in (UP, DOWN):
        for half in (0, 1):
            send(half, p, f, way, inside[way])
    send(0, p, f, X)
    send(1, p, f, Y)
    for half in (0, 1):
        send(half, p, f, SIB)

    for half, prompt, unit in ((0, p, owner(z, yo)), (1, q, f)):
        arrived(half, prompt, unit)
        for way in (UP, DOWN):
            send(half, prompt, unit, way, inside[way])
        send(half, prompt, unit, last[half])
        send(half, prompt, unit, SIB)

    def settle(layer, guard):
        def run():
            for half, prompt, column in ((0, q, y), (1, p, yo), (0, q, yo), (1, q, yo)):
                arrived(half, prompt, owner(layer, column))
                piece(half, prompt, owner(layer, column), SIB).start()
        for half, prompt, column in ((0, q, y), (1, p, yo), (0, q, yo), (1, q, yo)):
            started.append((guard, piece(half, prompt, owner(layer, column), SIB)))
        if guard is None:
            run()
        else:
            pl.when(guard)(run)

    def sources(step):
        return ((z - step, z - step >= 0, UP), (z + step, z + step < layers, DOWN))

    for step in range(1, layers):
        for half, prompt, column in ((0, p, y), (1, p, y), (0, p, yo), (1, q, y)):
            for layer, present, way in sources(step):
                unit = owner(layer, column)
                pl.when(present)(functools.partial(arrived, half, prompt, unit))
                send(half, prompt, unit, way, both(present, inside[way]))
                send(half, prompt, unit, last[half], present)
                send(half, prompt, unit, SIB, present)
        if step == 1:
            settle(z, None)
        else:
            for layer, present, _ in sources(step - 1):
                settle(layer, present)
    if layers == 1:
        settle(z, None)
    else:
        for layer, present, _ in sources(layers - 1):
            settle(layer, present)

    def scale(weights):
        return jnp.transpose(jnp.broadcast_to(weights[...], (LANES, slots)))[:, :1]

    def product(prompt, weights):
        rows = buf[prompt].reshape(slots, width)
        sums = lax.dot_general(
            rows, enc[...], (((1,), (1,)), ((), ())), preferred_element_type=jnp.float32
        )
        return (scale(weights) * sums).astype(out_ref.dtype)

    def from_sibling(prompt):
        for layer in range(layers):
            for column in range(COLUMNS):
                for half in (0, 1):
                    arrived(half, prompt, owner(layer, column, 1 - core))

    load_enc.wait()
    act_copy.wait()
    from_sibling(q)
    part[...] = product(q, act_other)
    mine = pl.ds(pl.multiple_of(p * targets, LANES), targets)
    back = pltpu.make_async_remote_copy(
        src_ref=part, dst_ref=out_ref.at[:, mine], send_sem=pair_send.at[1], recv_sem=pair_recv.at[1],
        device_id=places[X], device_id_type=MESH,
    )
    back.start()
    from_sibling(p)
    out_ref[:, mine] = product(p, act_ref)
    for guard, copy in started:
        if guard is None:
            copy.wait_send()
        else:
            pl.when(guard)(copy.wait_send)
    back.wait()


def moved_rows(prompts, owners, decoder, encoder, row_ids, counts, activity):
    own, width, targets = row_ids.shape[1], decoder.shape[1], encoder.shape[0]
    slots = owners * own
    edges = pl.pallas_call(
        functools.partial(kernel, owners // (COLUMNS * CORES)),
        out_shape=jax.ShapeDtypeStruct((slots, prompts * targets), jnp.bfloat16),
        in_specs=[
            pl.BlockSpec(memory_space=pltpu.SMEM),
            pl.BlockSpec(memory_space=pltpu.SMEM),
            pl.BlockSpec(memory_space=pltpu.VMEM),
            pl.BlockSpec(memory_space=pl.ANY),
            pl.BlockSpec(memory_space=pl.ANY),
        ],
        out_specs=pl.BlockSpec(memory_space=pltpu.VMEM),
        scratch_shapes=[
            pltpu.VMEM((prompts, owners, own, width), decoder.dtype),
            pltpu.VMEM(decoder.shape, decoder.dtype),
            pltpu.VMEM(encoder.shape, encoder.dtype),
            pltpu.VMEM(activity.shape, activity.dtype),
            pltpu.VMEM((slots, targets), jnp.bfloat16),
            pltpu.SemaphoreType.DMA((2,)),
            pltpu.SemaphoreType.DMA((2,)),
            pltpu.SemaphoreType.DMA((2,)),
            pltpu.SemaphoreType.DMA((5, 2, prompts, owners)),
            pltpu.SemaphoreType.DMA((2, prompts, owners)),
        ],
        compiler_params=pltpu.CompilerParams(
            collective_id=0, has_side_effects=True, vmem_limit_bytes=48 * 1024 * 1024
        ),
    )(row_ids, counts, activity, decoder, encoder)
    return edges[None]


def solution(mesh):
    prompts, owners = mesh.shape["prompt"], mesh.shape["feat"]
    if prompts == 2 and owners % (COLUMNS * CORES) == 0:
        per_device = functools.partial(moved_rows, prompts, owners)
    else:
        per_device = gathered_encoder
    in_specs = (
        P("feat", None),
        P(("feat", "prompt"), None),
        P("prompt", "feat"),
        P("prompt", None),
        P("prompt", None),
    )
    out_specs = P("prompt", None, "feat")
    return jax.shard_map(
        per_device, mesh=mesh, in_specs=in_specs, out_specs=out_specs, check_vma=False
    )
```

```python
import functools

import jax
import jax.numpy as jnp
from jax import lax
from jax.experimental import pallas as pl
from jax.experimental.pallas import tpu as pltpu
from jax.sharding import PartitionSpec as P

MESH = pl.DeviceIdType.MESH
LANES = 128
COLUMNS = 2
CORES = 2


def gathered_encoder(decoder, encoder, row_ids, counts, activity):
    slot_count = row_ids.shape[1]
    owner_index = lax.axis_index("feat")
    picked_rows = jnp.take(decoder, row_ids[0], axis=0)
    live_count = lax.dynamic_index_in_dim(counts[0], owner_index, 0, keepdims=False)
    live_slots = jnp.arange(slot_count, dtype=jnp.int32) < live_count
    source_rows = jnp.where(live_slots[:, None], picked_rows, jnp.zeros((), picked_rows.dtype))
    weights = activity[0]
    whole_rows = lax.all_gather(source_rows, "feat", axis=0, tiled=True)
    products = lax.dot_general(
        whole_rows,
        lax.all_gather(encoder, "prompt", axis=0, tiled=True),
        (((1,), (1,)), ((), ())),
        preferred_element_type=jnp.float32,
    )
    edges = (weights[:, None] * products).astype(jnp.bfloat16)
    return edges[None]


X, Y, UP, DOWN, SIB = range(5)


def kernel(
    layers, ids_hbm, counts_hbm, act_hbm, dec_hbm, enc_hbm, out_ref,
    buf, dec, enc, ids, counts, act, scale, part,
    small_sem, load_sem, act_send, act_recv, back_send, back_recv, send_sem, recv_sem,
):
    prompts, members, own, width = buf.shape[1:]
    targets = enc.shape[0]
    layer_slots = members * own
    half_width = width // LANES // 2 * LANES
    spans = (pl.ds(0, half_width), pl.ds(half_width, width - half_width))

    p = lax.axis_index("prompt")
    f = lax.axis_index("feat")
    core = f % CORES
    y = (f // CORES) % COLUMNS
    z = f // (CORES * COLUMNS)
    q, yo = 1 - p, 1 - y

    def owner(layer, column, which):
        return (layer * COLUMNS + column) * CORES + which

    places = {
        X: (q, f),
        Y: (p, owner(z, yo, core)),
        UP: (p, owner(z + 1, y, core)),
        DOWN: (p, owner(z - 1, y, core)),
        SIB: (p, owner(z, y, 1 - core)),
    }
    inside = {UP: z < layers - 1, DOWN: z > 0}

    load_small = [
        pltpu.make_async_copy(src, dst, small_sem.at[i])
        for i, (src, dst) in enumerate(((ids_hbm, ids), (counts_hbm, counts), (act_hbm, act.at[0])))
    ]
    load_dec = [
        pltpu.make_async_copy(dec_hbm.at[:, span], dec.at[:, span], load_sem.at[i])
        for i, span in enumerate(spans)
    ]
    load_enc = pltpu.make_async_copy(enc_hbm, enc, load_sem.at[2])
    for copy in load_small + load_dec:
        copy.start()

    barrier = pltpu.get_barrier_semaphore()
    for way in (X, Y, SIB):
        pl.semaphore_signal(barrier, inc=1, device_id=places[way], device_id_type=MESH)
    for way in (UP, DOWN):
        @pl.when(inside[way])
        def _():
            pl.semaphore_signal(barrier, inc=1, device_id=places[way], device_id_type=MESH)

    for copy in load_small:
        copy.wait()
    row_count = dec.shape[0]
    lane = lax.broadcasted_iota(jnp.int32, (own, row_count), 1)
    slot = lax.broadcasted_iota(jnp.int32, (own, row_count), 0)
    live = counts[0, f]
    wanted = jnp.full((own, row_count), -1, jnp.int32)
    for k in range(own):
        wanted = jnp.where(slot == k, jnp.where(k < live, ids[0, k], -1), wanted)
    one_hot = jnp.where(lane == wanted, 1.0, 0.0).astype(jnp.bfloat16)

    def pick(half):
        load_dec[half].wait()
        rows = jnp.dot(one_hot, dec[:, spans[half]], preferred_element_type=jnp.float32)
        buf[z, p, y * CORES + core, :, spans[half]] = rows.astype(buf.dtype)

    started = []

    def piece(half, prompt, layer, column, way, which=None):
        member = column * CORES + (core if which is None else which)
        ref = buf.at[layer, prompt, member, :, spans[half]]
        return pltpu.make_async_remote_copy(
            src_ref=ref, dst_ref=ref,
            send_sem=send_sem.at[way, half, layer, prompt, member],
            recv_sem=recv_sem.at[half, layer, prompt, member],
            device_id=places[way], device_id_type=MESH,
        )

    def send(half, prompt, layer, column, way, guard=None):
        copy = piece(half, prompt, layer, column, way)
        started.append((guard, copy))
        if guard is None:
            copy.start()
        else:
            pl.when(guard)(copy.start)

    def arrived(half, prompt, layer, column, which=None):
        piece(half, prompt, layer, column, SIB, which).wait_recv()

    def both(a, b):
        return jnp.logical_and(a, b)

    first, last = (Y, X), (X, Y)

    def launch(half):
        for way in (UP, DOWN):
            send(half, p, z, y, way, inside[way])
        send(half, p, z, y, first[half])
        send(half, p, z, y, last[half])
        send(half, p, z, y, SIB)

    pick(0)
    load_enc.start()
    peers = 3 + (z + layers - 1) // layers + (layers - 1 - z + layers - 1) // layers
    pl.semaphore_wait(barrier, peers)
    launch(0)
    pick(1)
    launch(1)
    act_copy = pltpu.make_async_remote_copy(
        src_ref=act.at[0], dst_ref=act.at[1], send_sem=act_send.at[0], recv_sem=act_recv.at[0],
        device_id=places[X], device_id_type=MESH,
    )
    act_copy.start()

    for half, prompt, column in ((0, p, yo), (1, q, y)):
        arrived(half, prompt, z, column)
        for way in (UP, DOWN):
            send(half, prompt, z, column, way, inside[way])
        send(half, prompt, z, column, last[half])
        send(half, prompt, z, column, SIB)

    for i in (0, 1):
        if i == 1:
            act_copy.wait()
        row = jnp.broadcast_to(act[i], (LANES, act.shape[2]))
        scale[i] = jnp.transpose(row)
    load_enc.wait()

    def sources(step):
        if step == 0:
            return ((z, None, None),)
        return ((z - step, z - step >= 0, UP), (z + step, z + step < layers, DOWN))

    def guarded(guard, run):
        if guard is None:
            run()
        else:
            pl.when(guard)(run)

    def settle(step):
        for layer, present, _ in sources(step):
            for half, prompt, column in ((0, q, y), (1, p, yo), (0, q, yo), (1, q, yo)):
                guarded(present, functools.partial(arrived, half, prompt, layer, column))
                send(half, prompt, layer, column, SIB, present)

    mine = pl.ds(pl.multiple_of(p * targets, LANES), targets)

    def back(layer):
        rows = pl.ds(pl.multiple_of(layer * layer_slots, layer_slots), layer_slots)
        return pltpu.make_async_remote_copy(
            src_ref=part.at[rows], dst_ref=out_ref.at[rows, mine],
            send_sem=back_send.at[layer], recv_sem=back_recv.at[layer],
            device_id=places[X], device_id_type=MESH,
        )

    def multiply(layer):
        for prompt in (q, p):
            for column in range(COLUMNS):
                for half in (0, 1):
                    arrived(half, prompt, layer, column, 1 - core)
        rows = pl.ds(pl.multiple_of(layer * layer_slots, layer_slots), layer_slots)
        sums = lax.dot_general(
            buf[layer].reshape(prompts * layer_slots, width), enc[...],
            (((1,), (1,)), ((), ())), preferred_element_type=jnp.float32,
        )
        lower, upper = sums[:layer_slots], sums[layer_slots:]
        here = jnp.where(p == 0, lower, upper)
        there = jnp.where(p == 0, upper, lower)
        part[rows, :] = (scale[1, rows, :1] * there).astype(part.dtype)
        back(layer).start()
        out_ref[rows, mine] = (scale[0, rows, :1] * here).astype(out_ref.dtype)

    def compute(step):
        for layer, present, _ in sources(step):
            guarded(present, functools.partial(multiply, layer))

    for step in range(1, layers):
        for n, (half, prompt, column) in enumerate(((0, p, y), (1, p, y), (0, p, yo), (1, q, y))):
            for layer, present, way in sources(step):
                pl.when(present)(functools.partial(arrived, half, prompt, layer, column))
                send(half, prompt, layer, column, way, both(present, inside[way]))
                send(half, prompt, layer, column, last[half], present)
                send(half, prompt, layer, column, SIB, present)
            if n == 1:
                settle(step - 1)
            if n == 2:
                compute(step - 1)
    settle(layers - 1)
    compute(layers - 1)

    for guard, copy in started:
        guarded(guard, copy.wait_send)
    for layer in range(layers):
        back(layer).wait()


def moved_rows(prompts, owners, decoder, encoder, row_ids, counts, activity):
    own, width, targets = row_ids.shape[1], decoder.shape[1], encoder.shape[0]
    members = COLUMNS * CORES
    layers, slots = owners // members, owners * own
    edges = pl.pallas_call(
        functools.partial(kernel, layers),
        out_shape=jax.ShapeDtypeStruct((slots, prompts * targets), jnp.bfloat16),
        in_specs=[pl.BlockSpec(memory_space=pl.ANY)] * 5,
        out_specs=pl.BlockSpec(memory_space=pltpu.VMEM),
        scratch_shapes=[
            pltpu.VMEM((layers, prompts, members, own, width), decoder.dtype),
            pltpu.VMEM(decoder.shape, decoder.dtype),
            pltpu.VMEM(encoder.shape, encoder.dtype),
            pltpu.SMEM(row_ids.shape, row_ids.dtype),
            pltpu.SMEM(counts.shape, counts.dtype),
            pltpu.VMEM((prompts,) + activity.shape, activity.dtype),
            pltpu.VMEM((prompts, slots, LANES), activity.dtype),
            pltpu.VMEM((slots, targets), jnp.bfloat16),
            pltpu.SemaphoreType.DMA((3,)),
            pltpu.SemaphoreType.DMA((3,)),
            pltpu.SemaphoreType.DMA((1,)),
            pltpu.SemaphoreType.DMA((1,)),
            pltpu.SemaphoreType.DMA((layers,)),
            pltpu.SemaphoreType.DMA((layers,)),
            pltpu.SemaphoreType.DMA((5, 2, layers, prompts, members)),
            pltpu.SemaphoreType.DMA((2, layers, prompts, members)),
        ],
        compiler_params=pltpu.CompilerParams(
            collective_id=0, has_side_effects=True, vmem_limit_bytes=58 * 1024 * 1024
        ),
    )(row_ids, counts, activity, decoder, encoder)
    return edges[None]


def solution(mesh):
    prompts, owners = mesh.shape["prompt"], mesh.shape["feat"]
    if prompts == 2 and owners % (COLUMNS * CORES) == 0:
        per_device = functools.partial(moved_rows, prompts, owners)
    else:
        per_device = gathered_encoder
    in_specs = (
        P("feat", None),
        P(("feat", "prompt"), None),
        P("prompt", "feat"),
        P("prompt", None),
        P("prompt", None),
    )
    out_specs = P("prompt", None, "feat")
    return jax.shard_map(
        per_device, mesh=mesh, in_specs=in_specs, out_specs=out_specs, check_vma=False
    )
```

```python
import functools

import jax
import jax.numpy as jnp
from jax import lax
from jax.experimental import pallas as pl
from jax.experimental.pallas import tpu as pltpu
from jax.sharding import PartitionSpec as P

MESH = pl.DeviceIdType.MESH
LANES = 128
COLUMNS = 2
CORES = 2


def gathered_encoder(decoder, encoder, row_ids, counts, activity):
    slot_count = row_ids.shape[1]
    owner_index = lax.axis_index("feat")
    picked_rows = jnp.take(decoder, row_ids[0], axis=0)
    live_count = lax.dynamic_index_in_dim(counts[0], owner_index, 0, keepdims=False)
    live_slots = jnp.arange(slot_count, dtype=jnp.int32) < live_count
    source_rows = jnp.where(live_slots[:, None], picked_rows, jnp.zeros((), picked_rows.dtype))
    weights = activity[0]
    whole_rows = lax.all_gather(source_rows, "feat", axis=0, tiled=True)
    products = lax.dot_general(
        whole_rows,
        lax.all_gather(encoder, "prompt", axis=0, tiled=True),
        (((1,), (1,)), ((), ())),
        preferred_element_type=jnp.float32,
    )
    edges = (weights[:, None] * products).astype(jnp.bfloat16)
    return edges[None]


X, Y, UP, DOWN, SIB = range(5)


def kernel(
    layers, ids_hbm, counts_hbm, act_hbm, dec_hbm, enc_hbm, out_ref,
    buf, dec, enc, ids, counts, act, scale, part,
    small_sem, load_sem, act_send, act_recv, back_send, back_recv, send_sem, recv_sem,
):
    prompts, members, own, width = buf.shape[1:]
    targets = enc.shape[0]
    layer_slots = members * own
    half_width = width // LANES // 2 * LANES
    spans = (pl.ds(0, half_width), pl.ds(half_width, width - half_width))

    p = lax.axis_index("prompt")
    f = lax.axis_index("feat")
    core = f % CORES
    y = (f // CORES) % COLUMNS
    z = f // (CORES * COLUMNS)
    q, yo = 1 - p, 1 - y

    def owner(layer, column, which):
        return (layer * COLUMNS + column) * CORES + which

    places = {
        X: (q, f),
        Y: (p, owner(z, yo, core)),
        UP: (p, owner(z + 1, y, core)),
        DOWN: (p, owner(z - 1, y, core)),
        SIB: (p, owner(z, y, 1 - core)),
    }
    inside = {UP: z < layers - 1, DOWN: z > 0}

    load_small = [
        pltpu.make_async_copy(src, dst, small_sem.at[i])
        for i, (src, dst) in enumerate(((ids_hbm, ids), (counts_hbm, counts), (act_hbm, act.at[0])))
    ]
    load_dec = [
        pltpu.make_async_copy(dec_hbm.at[:, span], dec.at[:, span], load_sem.at[i])
        for i, span in enumerate(spans)
    ]
    load_enc = pltpu.make_async_copy(enc_hbm, enc, load_sem.at[2])
    for copy in load_small + load_dec:
        copy.start()

    barrier = pltpu.get_barrier_semaphore()
    for way in (X, Y, SIB):
        pl.semaphore_signal(barrier, inc=1, device_id=places[way], device_id_type=MESH)
    for way in (UP, DOWN):
        @pl.when(inside[way])
        def _():
            pl.semaphore_signal(barrier, inc=1, device_id=places[way], device_id_type=MESH)

    for copy in load_small:
        copy.wait()
    row_count = dec.shape[0]
    lane = lax.broadcasted_iota(jnp.int32, (own, row_count), 1)
    slot = lax.broadcasted_iota(jnp.int32, (own, row_count), 0)
    live = counts[0, f]
    wanted = jnp.full((own, row_count), -1, jnp.int32)
    for k in range(own):
        wanted = jnp.where(slot == k, jnp.where(k < live, ids[0, k], -1), wanted)
    one_hot = jnp.where(lane == wanted, 1.0, 0.0).astype(jnp.bfloat16)

    def pick(half):
        load_dec[half].wait()
        rows = jnp.dot(one_hot, dec[:, spans[half]], preferred_element_type=jnp.float32)
        buf[z, p, y * CORES + core, :, spans[half]] = rows.astype(buf.dtype)

    started = []

    def piece(half, prompt, layer, column, way, which=None):
        member = column * CORES + (core if which is None else which)
        ref = buf.at[layer, prompt, member, :, spans[half]]
        return pltpu.make_async_remote_copy(
            src_ref=ref, dst_ref=ref,
            send_sem=send_sem.at[way, half, layer, prompt, member],
            recv_sem=recv_sem.at[half, layer, prompt, member],
            device_id=places[way], device_id_type=MESH,
        )

    def send(half, prompt, layer, column, way, guard=None):
        copy = piece(half, prompt, layer, column, way)
        started.append((guard, copy))
        if guard is None:
            copy.start()
        else:
            pl.when(guard)(copy.start)

    def arrived(half, prompt, layer, column, which=None):
        piece(half, prompt, layer, column, SIB, which).wait_recv()

    def both(a, b):
        return jnp.logical_and(a, b)

    first, last = (Y, X), (X, Y)

    def launch(half):
        for way in (UP, DOWN):
            send(half, p, z, y, way, inside[way])
        send(half, p, z, y, first[half])
        send(half, p, z, y, last[half])
        send(half, p, z, y, SIB)

    pick(0)
    load_enc.start()
    peers = 3 + (z + layers - 1) // layers + (layers - 1 - z + layers - 1) // layers
    pl.semaphore_wait(barrier, peers)
    launch(0)
    pick(1)
    launch(1)
    act_copy = pltpu.make_async_remote_copy(
        src_ref=act.at[0], dst_ref=act.at[1], send_sem=act_send.at[0], recv_sem=act_recv.at[0],
        device_id=places[X], device_id_type=MESH,
    )
    act_copy.start()

    for half, prompt, column in ((0, p, yo), (1, q, y)):
        arrived(half, prompt, z, column)
        for way in (UP, DOWN):
            send(half, prompt, z, column, way, inside[way])
        send(half, prompt, z, column, last[half])
        send(half, prompt, z, column, SIB)

    for i in (0, 1):
        if i == 1:
            act_copy.wait()
        row = jnp.broadcast_to(act[i], (LANES, act.shape[2]))
        scale[i] = jnp.transpose(row)
    load_enc.wait()

    def sources(step):
        if step == 0:
            return ((z, None, None),)
        return ((z - step, z - step >= 0, UP), (z + step, z + step < layers, DOWN))

    def guarded(guard, run):
        if guard is None:
            run()
        else:
            pl.when(guard)(run)

    def settle(step):
        for layer, present, _ in sources(step):
            for half, prompt, column in ((0, q, y), (1, p, yo), (0, q, yo), (1, q, yo)):
                guarded(present, functools.partial(arrived, half, prompt, layer, column))
                send(half, prompt, layer, column, SIB, present)

    mine = pl.ds(pl.multiple_of(p * targets, LANES), targets)

    def back(layer):
        rows = pl.ds(pl.multiple_of(layer * layer_slots, layer_slots), layer_slots)
        return pltpu.make_async_remote_copy(
            src_ref=part.at[rows], dst_ref=out_ref.at[rows, mine],
            send_sem=back_send.at[layer], recv_sem=back_recv.at[layer],
            device_id=places[X], device_id_type=MESH,
        )

    def multiply(layer):
        for prompt in (q, p):
            for column in range(COLUMNS):
                for half in (0, 1):
                    arrived(half, prompt, layer, column, 1 - core)
        rows = pl.ds(pl.multiple_of(layer * layer_slots, layer_slots), layer_slots)
        sums = lax.dot_general(
            buf[layer].reshape(prompts * layer_slots, width), enc[...],
            (((1,), (1,)), ((), ())), preferred_element_type=jnp.float32,
        )
        lower, upper = sums[:layer_slots], sums[layer_slots:]
        here = jnp.where(p == 0, lower, upper)
        there = jnp.where(p == 0, upper, lower)
        part[rows, :] = (scale[1, rows, :1] * there).astype(part.dtype)
        back(layer).start()
        out_ref[rows, mine] = (scale[0, rows, :1] * here).astype(out_ref.dtype)

    def compute(step):
        for layer, present, _ in sources(step):
            guarded(present, functools.partial(multiply, layer))

    for step in range(1, layers):
        for half, prompt, column in ((0, p, y), (1, p, y), (0, p, yo), (1, q, y)):
            for layer, present, way in sources(step):
                pl.when(present)(functools.partial(arrived, half, prompt, layer, column))
                send(half, prompt, layer, column, way, both(present, inside[way]))
                send(half, prompt, layer, column, last[half], present)
                send(half, prompt, layer, column, SIB, present)
        settle(step - 1)
        compute(step - 1)
    settle(layers - 1)
    compute(layers - 1)

    for guard, copy in started:
        guarded(guard, copy.wait_send)
    for layer in range(layers):
        back(layer).wait()


def moved_rows(prompts, owners, decoder, encoder, row_ids, counts, activity):
    own, width, targets = row_ids.shape[1], decoder.shape[1], encoder.shape[0]
    members = COLUMNS * CORES
    layers, slots = owners // members, owners * own
    edges = pl.pallas_call(
        functools.partial(kernel, layers),
        out_shape=jax.ShapeDtypeStruct((slots, prompts * targets), jnp.bfloat16),
        in_specs=[pl.BlockSpec(memory_space=pl.ANY)] * 5,
        out_specs=pl.BlockSpec(memory_space=pltpu.VMEM),
        scratch_shapes=[
            pltpu.VMEM((layers, prompts, members, own, width), decoder.dtype),
            pltpu.VMEM(decoder.shape, decoder.dtype),
            pltpu.VMEM(encoder.shape, encoder.dtype),
            pltpu.SMEM(row_ids.shape, row_ids.dtype),
            pltpu.SMEM(counts.shape, counts.dtype),
            pltpu.VMEM((prompts,) + activity.shape, activity.dtype),
            pltpu.VMEM((prompts, slots, LANES), activity.dtype),
            pltpu.VMEM((slots, targets), jnp.bfloat16),
            pltpu.SemaphoreType.DMA((3,)),
            pltpu.SemaphoreType.DMA((3,)),
            pltpu.SemaphoreType.DMA((1,)),
            pltpu.SemaphoreType.DMA((1,)),
            pltpu.SemaphoreType.DMA((layers,)),
            pltpu.SemaphoreType.DMA((layers,)),
            pltpu.SemaphoreType.DMA((5, 2, layers, prompts, members)),
            pltpu.SemaphoreType.DMA((2, layers, prompts, members)),
        ],
        compiler_params=pltpu.CompilerParams(
            collective_id=0, has_side_effects=True, vmem_limit_bytes=58 * 1024 * 1024
        ),
    )(row_ids, counts, activity, decoder, encoder)
    return edges[None]


def solution(mesh):
    prompts, owners = mesh.shape["prompt"], mesh.shape["feat"]
    if prompts == 2 and owners % (COLUMNS * CORES) == 0:
        per_device = functools.partial(moved_rows, prompts, owners)
    else:
        per_device = gathered_encoder
    in_specs = (
        P("feat", None),
        P(("feat", "prompt"), None),
        P("prompt", "feat"),
        P("prompt", None),
        P("prompt", None),
    )
    out_specs = P("prompt", None, "feat")
    return jax.shard_map(
        per_device, mesh=mesh, in_specs=in_specs, out_specs=out_specs, check_vma=False
    )
```

```python
import functools

import jax
import jax.numpy as jnp
from jax import lax
from jax.experimental import pallas as pl
from jax.experimental.pallas import tpu as pltpu
from jax.sharding import PartitionSpec as P

MESH = pl.DeviceIdType.MESH
LANES = 128
COLUMNS = 2
CORES = 2


def gathered_encoder(decoder, encoder, row_ids, counts, activity):
    slot_count = row_ids.shape[1]
    owner_index = lax.axis_index("feat")
    picked_rows = jnp.take(decoder, row_ids[0], axis=0)
    live_count = lax.dynamic_index_in_dim(counts[0], owner_index, 0, keepdims=False)
    live_slots = jnp.arange(slot_count, dtype=jnp.int32) < live_count
    source_rows = jnp.where(live_slots[:, None], picked_rows, jnp.zeros((), picked_rows.dtype))
    weights = activity[0]
    whole_rows = lax.all_gather(source_rows, "feat", axis=0, tiled=True)
    products = lax.dot_general(
        whole_rows,
        lax.all_gather(encoder, "prompt", axis=0, tiled=True),
        (((1,), (1,)), ((), ())),
        preferred_element_type=jnp.float32,
    )
    edges = (weights[:, None] * products).astype(jnp.bfloat16)
    return edges[None]


X, Y, UP, DOWN, SIB = range(5)


def kernel(
    layers, ids_hbm, counts_hbm, act_hbm, dec_hbm, enc_hbm, out_ref,
    buf, dec, enc, ids, counts, act, scale, part,
    small_sem, load_sem, act_send, act_recv, back_send, back_recv, send_sem, recv_sem,
):
    prompts, members, own, width = buf.shape[1:]
    targets = enc.shape[0]
    layer_slots = members * own
    half_width = width // LANES // 2 * LANES
    spans = (pl.ds(0, half_width), pl.ds(half_width, width - half_width))

    p = lax.axis_index("prompt")
    f = lax.axis_index("feat")
    core = f % CORES
    y = (f // CORES) % COLUMNS
    z = f // (CORES * COLUMNS)
    q, yo = 1 - p, 1 - y

    def owner(layer, column, which):
        return (layer * COLUMNS + column) * CORES + which

    places = {
        X: (q, f),
        Y: (p, owner(z, yo, core)),
        UP: (p, owner(z + 1, y, core)),
        DOWN: (p, owner(z - 1, y, core)),
        SIB: (p, owner(z, y, 1 - core)),
    }
    inside = {UP: z < layers - 1, DOWN: z > 0}

    load_small = [
        pltpu.make_async_copy(src, dst, small_sem.at[i])
        for i, (src, dst) in enumerate(((ids_hbm, ids), (counts_hbm, counts), (act_hbm, act.at[0])))
    ]
    load_dec = [
        pltpu.make_async_copy(dec_hbm.at[:, span], dec.at[:, span], load_sem.at[i])
        for i, span in enumerate(spans)
    ]
    load_enc = pltpu.make_async_copy(enc_hbm, enc, load_sem.at[2])
    for copy in load_small + load_dec:
        copy.start()

    barrier = pltpu.get_barrier_semaphore()
    for way in (X, Y, SIB):
        pl.semaphore_signal(barrier, inc=1, device_id=places[way], device_id_type=MESH)
    for way in (UP, DOWN):
        @pl.when(inside[way])
        def _():
            pl.semaphore_signal(barrier, inc=1, device_id=places[way], device_id_type=MESH)

    for copy in load_small:
        copy.wait()
    row_count = dec.shape[0]
    lane = lax.broadcasted_iota(jnp.int32, (own, row_count), 1)
    slot = lax.broadcasted_iota(jnp.int32, (own, row_count), 0)
    live = counts[0, f]
    wanted = jnp.full((own, row_count), -1, jnp.int32)
    for k in range(own):
        wanted = jnp.where(slot == k, jnp.where(k < live, ids[0, k], -1), wanted)
    one_hot = jnp.where(lane == wanted, 1.0, 0.0).astype(jnp.bfloat16)

    def pick(half):
        load_dec[half].wait()
        rows = jnp.dot(one_hot, dec[:, spans[half]], preferred_element_type=jnp.float32)
        buf[z, p, y * CORES + core, :, spans[half]] = rows.astype(buf.dtype)

    started = []

    def piece(half, prompt, layer, column, way, which=None):
        member = column * CORES + (core if which is None else which)
        ref = buf.at[layer, prompt, member, :, spans[half]]
        return pltpu.make_async_remote_copy(
            src_ref=ref, dst_ref=ref,
            send_sem=send_sem.at[way, half, layer, prompt, member],
            recv_sem=recv_sem.at[half, layer, prompt, member],
            device_id=places[way], device_id_type=MESH,
        )

    def send(half, prompt, layer, column, way, guard=None):
        copy = piece(half, prompt, layer, column, way)
        started.append((guard, copy))
        if guard is None:
            copy.start()
        else:
            pl.when(guard)(copy.start)

    def arrived(half, prompt, layer, column, which=None):
        piece(half, prompt, layer, column, SIB, which).wait_recv()

    def both(a, b):
        return jnp.logical_and(a, b)

    first, last = (Y, X), (X, Y)

    def launch(half):
        for way in (UP, DOWN):
            send(half, p, z, y, way, inside[way])
        send(half, p, z, y, first[half])
        send(half, p, z, y, last[half])
        send(half, p, z, y, SIB)

    pick(0)
    load_enc.start()
    peers = 3 + (z + layers - 1) // layers + (layers - 1 - z + layers - 1) // layers
    pl.semaphore_wait(barrier, peers)
    launch(0)
    pick(1)
    launch(1)
    act_copy = pltpu.make_async_remote_copy(
        src_ref=act.at[0], dst_ref=act.at[1], send_sem=act_send.at[0], recv_sem=act_recv.at[0],
        device_id=places[X], device_id_type=MESH,
    )
    act_copy.start()

    for half, prompt, column in ((0, p, yo), (1, q, y)):
        arrived(half, prompt, z, column)
        for way in (UP, DOWN):
            send(half, prompt, z, column, way, inside[way])
        send(half, prompt, z, column, last[half])
        send(half, prompt, z, column, SIB)

    for i in (0, 1):
        if i == 1:
            act_copy.wait()
        row = jnp.broadcast_to(act[i], (LANES, act.shape[2]))
        scale[i] = jnp.transpose(row)
    load_enc.wait()

    def sources(step):
        if step == 0:
            return ((z, None, None),)
        return ((z - step, z - step >= 0, UP), (z + step, z + step < layers, DOWN))

    def guarded(guard, run):
        if guard is None:
            run()
        else:
            pl.when(guard)(run)

    def settle(step):
        for layer, present, _ in sources(step):
            for half, prompt, column in ((0, q, y), (1, p, yo), (0, q, yo), (1, q, yo)):
                guarded(present, functools.partial(arrived, half, prompt, layer, column))
                send(half, prompt, layer, column, SIB, present)

    mine = pl.ds(pl.multiple_of(p * targets, LANES), targets)

    def back(layer):
        rows = pl.ds(pl.multiple_of(layer * layer_slots, layer_slots), layer_slots)
        return pltpu.make_async_remote_copy(
            src_ref=part.at[rows], dst_ref=out_ref.at[rows, mine],
            send_sem=back_send.at[layer], recv_sem=back_recv.at[layer],
            device_id=places[X], device_id_type=MESH,
        )

    def multiply(layer):
        for prompt in (q, p):
            for column in range(COLUMNS):
                for half in (0, 1):
                    arrived(half, prompt, layer, column, 1 - core)
        rows = pl.ds(pl.multiple_of(layer * layer_slots, layer_slots), layer_slots)
        sums = lax.dot_general(
            buf[layer].reshape(prompts * layer_slots, width), enc[...],
            (((1,), (1,)), ((), ())), preferred_element_type=jnp.float32,
        )
        lower, upper = sums[:layer_slots], sums[layer_slots:]
        here = jnp.where(p == 0, lower, upper)
        there = jnp.where(p == 0, upper, lower)
        part[rows, :] = (scale[1, rows, :1] * there).astype(part.dtype)
        back(layer).start()
        out_ref[rows, mine] = (scale[0, rows, :1] * here).astype(out_ref.dtype)

    def multiply_apart(layer):
        rows = pl.ds(pl.multiple_of(layer * layer_slots, layer_slots), layer_slots)
        for prompt in (q, p):
            for column in range(COLUMNS):
                for half in (0, 1):
                    arrived(half, prompt, layer, column, 1 - core)
            sums = lax.dot_general(
                buf[layer, prompt].reshape(layer_slots, width), enc[...],
                (((1,), (1,)), ((), ())), preferred_element_type=jnp.float32,
            )
            if prompt is q:
                part[rows, :] = (scale[1, rows, :1] * sums).astype(part.dtype)
                back(layer).start()
            else:
                out_ref[rows, mine] = (scale[0, rows, :1] * sums).astype(out_ref.dtype)

    def compute(step):
        run = multiply_apart if step == layers - 1 else multiply
        for layer, present, _ in sources(step):
            guarded(present, functools.partial(run, layer))

    for step in range(1, layers):
        for half, prompt, column in ((0, p, y), (1, p, y), (0, p, yo), (1, q, y)):
            for layer, present, way in sources(step):
                pl.when(present)(functools.partial(arrived, half, prompt, layer, column))
                send(half, prompt, layer, column, way, both(present, inside[way]))
                send(half, prompt, layer, column, last[half], present)
                send(half, prompt, layer, column, SIB, present)
        settle(step - 1)
        compute(step - 1)
    settle(layers - 1)
    compute(layers - 1)

    for guard, copy in started:
        guarded(guard, copy.wait_send)
    for layer in range(layers):
        back(layer).wait()


def moved_rows(prompts, owners, decoder, encoder, row_ids, counts, activity):
    own, width, targets = row_ids.shape[1], decoder.shape[1], encoder.shape[0]
    members = COLUMNS * CORES
    layers, slots = owners // members, owners * own
    edges = pl.pallas_call(
        functools.partial(kernel, layers),
        out_shape=jax.ShapeDtypeStruct((slots, prompts * targets), jnp.bfloat16),
        in_specs=[pl.BlockSpec(memory_space=pl.ANY)] * 5,
        out_specs=pl.BlockSpec(memory_space=pltpu.VMEM),
        scratch_shapes=[
            pltpu.VMEM((layers, prompts, members, own, width), decoder.dtype),
            pltpu.VMEM(decoder.shape, decoder.dtype),
            pltpu.VMEM(encoder.shape, encoder.dtype),
            pltpu.SMEM(row_ids.shape, row_ids.dtype),
            pltpu.SMEM(counts.shape, counts.dtype),
            pltpu.VMEM((prompts,) + activity.shape, activity.dtype),
            pltpu.VMEM((prompts, slots, LANES), activity.dtype),
            pltpu.VMEM((slots, targets), jnp.bfloat16),
            pltpu.SemaphoreType.DMA((3,)),
            pltpu.SemaphoreType.DMA((3,)),
            pltpu.SemaphoreType.DMA((1,)),
            pltpu.SemaphoreType.DMA((1,)),
            pltpu.SemaphoreType.DMA((layers,)),
            pltpu.SemaphoreType.DMA((layers,)),
            pltpu.SemaphoreType.DMA((5, 2, layers, prompts, members)),
            pltpu.SemaphoreType.DMA((2, layers, prompts, members)),
        ],
        compiler_params=pltpu.CompilerParams(
            collective_id=0, has_side_effects=True, vmem_limit_bytes=58 * 1024 * 1024
        ),
    )(row_ids, counts, activity, decoder, encoder)
    return edges[None]


def solution(mesh):
    prompts, owners = mesh.shape["prompt"], mesh.shape["feat"]
    if prompts == 2 and owners % (COLUMNS * CORES) == 0:
        per_device = functools.partial(moved_rows, prompts, owners)
    else:
        per_device = gathered_encoder
    in_specs = (
        P("feat", None),
        P(("feat", "prompt"), None),
        P("prompt", "feat"),
        P("prompt", None),
        P("prompt", None),
    )
    out_specs = P("prompt", None, "feat")
    return jax.shard_map(
        per_device, mesh=mesh, in_specs=in_specs, out_specs=out_specs, check_vma=False
    )
```
